128 devices in a mesh: grp: 4 (over y_hi, core), pan: 32 (over x, y_lo, z).
Axes of the slice: x: 4, y: 4 (y_hi: 2, y_lo: 2; y = y_hi * 2 + y_lo), z: 4, core: 2. Of those that a mesh axis runs over, the one named last changes fastest.
Arguments:
- assembled: bfloat16 [65536, 1536], P(('grp', 'pan')), may hold values from -6 to 6
- dest_group: int32 [128, 8], P(('grp', 'pan')), may hold values from 0 to 3, as said below
- block_mask: int32 [1024, 24], P(('grp', 'pan')), may hold values 0 or 1
Outputs:
- sign_rows: float32 [65536, 1536], P(('grp', 'pan'))
The draws below stay inside these ranges and needn't reach their ends.
Inputs may be any that keep to these rules, and one draw needn't show every extreme that they name: `dest_group`: each device's 8 entries name every region equally often.
All inputs are finite; a program needn't handle non-finite values. No bound on the sum of `block_mask` on one device may be relied on, other than what follows from the above.
Results may differ from the reference program's by a relative error of at most 0.0049.
Values may be sent and summed in bfloat16 or wider, within the bound.
A program may use at most 64 MiB of HBM per device.

```python
import jax
import jax.numpy as jnp
from jax import lax

ATOM = 64
CB = 8
ITERS = 2
TILE = 512
ROWS = 65536
N_GRP = 4
N_PAN = 32


def draw_dest_group(key, part):
    key = jax.random.fold_in(key, 11)
    scores = jax.random.randint(key, (N_GRP * N_PAN, CB), 0, 1 << 20)
    scores = scores * CB + jnp.arange(CB, dtype=jnp.int32)[None, :]
    ranking = jnp.argsort(scores, axis=1, stable=True).astype(jnp.int32)
    return (ranking // (CB // N_GRP)).astype(jnp.int32)


def plant(values, own_key, low, top_value):
    spot = [jax.random.randint(jax.random.fold_in(own_key, axis), (), 0, length) for axis, length in enumerate(values.shape)]
    widest = values.shape.index(max(values.shape))
    beside = spot[:widest] + [(spot[widest] + 1) % values.shape[widest]] + spot[widest + 1:]
    return values.at[tuple(spot)].set(low).at[tuple(beside)].set(top_value)


def steps_of(stream_key, shape, cuts, smallest, top_value):
    gain, own = 1.0, jax.random.fold_in(stream_key, 6)
    for axis_at, blocks in cuts:
        steps = jnp.exp(jax.random.uniform(jax.random.fold_in(own, axis_at), (blocks,), jnp.float32, smallest / len(cuts), top_value / len(cuts)))
        gain = gain * jnp.repeat(steps, shape[axis_at] // blocks).reshape([-1 if axis == axis_at else 1 for axis in range(len(shape))])
    return gain


def centred(rng, dims, scale, reach, cuts=(), held_as=jnp.bfloat16):
    array = scale * jax.random.normal(rng, dims, jnp.float32)
    if cuts:
        array = array * steps_of(rng, dims, cuts, -0.22, 0.18)
    return jnp.clip(array, -reach, reach).astype(held_as)


def setup_inputs(seed: int = 0) -> dict:
    streams_of = jax.random.split(jax.random.key(seed), 4)
    return {
        "assembled": centred(streams_of[0], (ROWS, 3 * TILE), 1.4, 6.0, ((0, 128),)),
        "dest_group": draw_dest_group(jax.random.fold_in(streams_of[3], 71), 0),
        "block_mask": plant((jax.random.randint(streams_of[2], (N_GRP * N_PAN * CB, 3 * CB), 0, 4) < 3).astype(jnp.int32), jax.random.fold_in(streams_of[2], 1), 0, 1),
    }


def band_region(pair):
    first, second = pair
    tile_rows = first.shape[1]
    one_side = first.astype(jnp.float32)
    lower_rows = jnp.roll(second, 1, axis=0)[:, :, tile_rows:].astype(jnp.float32)
    upper_rows = jnp.roll(second, -1, axis=0)[:, :, :2 * tile_rows].astype(jnp.float32)
    summed = jnp.einsum("pik,pkj->pij", one_side[:, :, tile_rows:2 * tile_rows], second.astype(jnp.float32))
    summed = summed.at[:, :, :2 * tile_rows].add(jnp.einsum("pik,pkj->pij", one_side[:, :, :tile_rows], lower_rows))
    summed = summed.at[:, :, tile_rows:].add(jnp.einsum("pik,pkj->pij", one_side[:, :, 2 * tile_rows:], upper_rows))
    return summed


def band_product(first, second):
    return lax.map(band_region, (first, second))


def reference(assembled, dest_group, block_mask):
    tile_rows = CB * ATOM
    band_cols = 3 * tile_rows
    blocks_all = assembled.reshape(N_GRP, N_PAN, CB, ATOM, band_cols)
    row_order = jnp.argsort(dest_group.reshape(N_GRP, N_PAN, CB), axis=2, stable=True).astype(jnp.int32)
    sorted_rows = jnp.take_along_axis(blocks_all, row_order[:, :, :, None, None], axis=2)
    sorted_rows = sorted_rows.reshape(N_GRP, N_PAN, N_GRP, (CB // N_GRP) * ATOM, band_cols)
    owned_rows = jnp.transpose(sorted_rows, (2, 1, 0, 3, 4)).reshape(N_GRP, N_PAN, tile_rows, band_cols)
    keep_mask = jnp.broadcast_to(block_mask.reshape(N_GRP, N_PAN, CB, 1, 3 * CB, 1), (N_GRP, N_PAN, CB, ATOM, 3 * CB, ATOM))
    keep_mask = keep_mask.reshape(N_GRP, N_PAN, tile_rows, band_cols).astype(jnp.float32)
    current = owned_rows * keep_mask.astype(jnp.bfloat16)
    row_index = jnp.arange(tile_rows)[:, None]
    col_index = jnp.arange(band_cols)[None, :]
    identity = (col_index == row_index + tile_rows).astype(jnp.float32)
    result = None
    for sweep in range(ITERS):
        square = keep_mask * band_product(current, current)
        factor = (3.0 * identity - square / (3.0 * tile_rows)).astype(jnp.bfloat16)
        result = 0.5 * keep_mask * band_product(current, factor)
        if sweep + 1 < ITERS:
            current = result.astype(jnp.bfloat16)
    return result.reshape(N_GRP * N_PAN * tile_rows, band_cols)
```

```python
import jax
import jax.numpy as jnp
from jax import lax
from jax.experimental import pallas as pl
from jax.experimental.pallas import tpu as pltpu
from jax.sharding import PartitionSpec as P

MESH = pl.DeviceIdType.MESH
ATOM = 64
CB = 8
T = ATOM * CB
CHUNK = 2 * ATOM
H = 256
BF = jnp.bfloat16
F32 = jnp.float32


def kernel(
    x_ref, dest_ref, mask_ref, out_ref,
    srt, land, mine, mask_l, mask_r, keep, keep_um, keep_lp,
    a_row, a_hl, a_hr, f_row, f_um, f_lp, f_dm, f_dp,
    b_row, b_hl, b_hr, h_row, h_um, h_lp, h_dm, h_dp,
    go_s, go_r, halo_s, halo_r, tile_s, tile_r, m_s, m_r,
):
    g = lax.axis_index("grp")
    p = lax.axis_index("pan")
    n = lax.axis_size("pan")
    core = lax.rem(g, 2)
    sib = g + 1 - 2 * core
    far = lax.rem(g + 2, 4)
    far_sib = lax.rem(sib + 2, 4)
    partners = (g, sib, far, far_sib)
    left = (g, lax.rem(p + n - 1, n))
    right = (g, lax.rem(p + 1, n))

    barrier = pltpu.get_barrier_semaphore()
    for other in partners[1:]:
        pl.semaphore_signal(barrier, inc=1, device_id=(other, p), device_id_type=MESH)
    for other in (left, right):
        pl.semaphore_signal(barrier, inc=1, device_id=other, device_id_type=MESH)

    def one_hot(rows, cols, of_row, of_col):
        row = of_row(lax.broadcasted_iota(jnp.int32, (rows, cols), 0))
        return (row == of_col(lax.broadcasted_iota(jnp.int32, (rows, cols), 1))).astype(F32)

    eye = one_hot(CB, CB, lambda v: v, lambda v: v)
    lane = lax.broadcasted_iota(jnp.int32, (1, CB), 1)
    key_row = (dest_ref[...] * CB + lane).astype(F32)
    key_col = jnp.sum(eye * key_row, axis=1, keepdims=True)
    rank = jnp.sum((key_col < key_row).astype(F32), axis=0, keepdims=True)
    spread = one_hot(CB, T, lambda v: v, lambda v: v // ATOM)
    slot = jnp.sum(spread * jnp.sum(eye * rank, axis=1, keepdims=True), axis=0, keepdims=True)
    slot = slot * ATOM + (lax.broadcasted_iota(jnp.int32, (1, T), 1) % ATOM).astype(F32)

    def gather(r):
        want = (partners[r] * CHUNK + lax.broadcasted_iota(jnp.int32, (CHUNK, T), 0)).astype(F32)
        pick = (want == slot).astype(BF)
        srt[r] = jnp.dot(pick, x_ref[...], preferred_element_type=F32).astype(BF)

    for r in (2, 3, 1, 0):
        gather(r)
    mine[...] = jnp.zeros_like(mine)
    mine[:, : 3 * CB] = mask_ref[...].astype(F32)
    pl.semaphore_wait(barrier, 5)

    def remote(src, dst, ss, rs, to):
        copy = pltpu.make_async_remote_copy(
            src_ref=src, dst_ref=dst, send_sem=ss, recv_sem=rs, device_id=to, device_id_type=MESH
        )
        copy.start()
        return copy

    pending = []
    arrive = {}
    my_rows = pl.multiple_of(g * CHUNK, CHUNK)
    for t in range(2):
        for r in (2, 3, 1):
            copy = remote(
                srt.at[r, pl.ds(t * ATOM, ATOM)],
                land.at[pl.ds(pl.multiple_of(my_rows + t * ATOM, ATOM), ATOM)],
                go_s.at[r, t], go_r.at[r, t], (partners[r], p),
            )
            arrive[r, t] = copy
    pending.append(remote(mine, mask_l, m_s.at[0], m_r.at[0], right))
    pending.append(remote(mine, mask_r, m_s.at[1], m_r.at[1], left))

    def expand(block, dst):
        rows = block.shape[0] * ATOM
        cols = block.shape[1] * ATOM
        up = (lax.broadcasted_iota(jnp.int32, (rows, CB), 0) // ATOM) == lax.broadcasted_iota(jnp.int32, (rows, CB), 1)
        across = lax.broadcasted_iota(jnp.int32, (block.shape[1], cols), 0) == (
            lax.broadcasted_iota(jnp.int32, (block.shape[1], cols), 1) // ATOM
        )
        tall = jnp.dot(up.astype(BF), block.astype(BF), preferred_element_type=F32)
        dst[...] = jnp.dot(tall.astype(BF), across.astype(BF), preferred_element_type=F32).astype(BF)

    expand(mine[:, : 3 * CB], keep)

    halo = {}

    def place(r, t):
        rows = pl.ds(pl.multiple_of(partners[r] * CHUNK + t * ATOM, ATOM), ATOM)
        if r == 0:
            a_row[rows, :] = srt[0, t * ATOM : (t + 1) * ATOM, :] * keep[rows, :]
        else:
            arrive[r, t].wait_recv()
            a_row[rows, :] = land[rows, :] * keep[rows, :]
        halo[0, r, t] = remote(
            a_row.at[rows, pl.ds(T, 2 * T)], a_hl.at[rows], halo_s.at[0, r, t], halo_r.at[0, r, t], right
        )
        halo[1, r, t] = remote(
            a_row.at[rows, pl.ds(0, 2 * T)], a_hr.at[rows], halo_s.at[1, r, t], halo_r.at[1, r, t], left
        )

    order = ((0, 0), (0, 1), (1, 0), (1, 1), (2, 0), (3, 0), (2, 1), (3, 1))
    for r, t in order:
        place(r, t)

    pending[0].wait_recv()
    pending[1].wait_recv()
    expand(mask_l[:, 2 * CB : 3 * CB], keep_um)
    expand(mask_r[:, :CB], keep_lp)
    for r, t in order:
        for side in (0, 1):
            halo[side, r, t].wait_recv()

    def tile_of(ref, k):
        return ref.at[:, pl.ds(k * T, T)]

    def product(pairs, finish):
        for i in range(T // H):
            for j in range(T // H):
                acc = None
                for a, b in pairs:
                    part = jnp.dot(
                        a[i * H : (i + 1) * H, :], b[:, j * H : (j + 1) * H], preferred_element_type=F32
                    )
                    acc = part if acc is None else acc + part
                finish(i, j, acc)

    def to_factor(dst, mask, diagonal):
        def finish(i, j, acc):
            at = (slice(i * H, (i + 1) * H), slice(j * H, (j + 1) * H))
            value = acc * mask[at].astype(F32) * (-1.0 / (3.0 * T))
            if diagonal and i == j:
                same = lax.broadcasted_iota(jnp.int32, (H, H), 0) == lax.broadcasted_iota(jnp.int32, (H, H), 1)
                value = jnp.where(same, 3.0 + value, value)
            dst[at] = value.astype(BF)

        return finish

    def to_next(dst, mask, dtype):
        def finish(i, j, acc):
            at = (slice(i * H, (i + 1) * H), slice(j * H, (j + 1) * H))
            dst[at] = (0.5 * acc * mask[at].astype(F32)).astype(dtype)

        return finish

    k_l, k_d, k_u = (tile_of(keep, k) for k in range(3))

    def tiles(row, um_ref, lp_ref, dm_ref, dp_ref):
        return dict(l=tile_of(row, 0), d=tile_of(row, 1), u=tile_of(row, 2), um=um_ref, lp=lp_ref, dm=dm_ref, dp=dp_ref)

    a = tiles(a_row, tile_of(a_hl, 1), tile_of(a_hr, 0), tile_of(a_hl, 0), tile_of(a_hr, 1))
    b = tiles(b_row, tile_of(b_hl, 1), tile_of(b_hr, 0), tile_of(b_hl, 0), tile_of(b_hr, 1))
    f = tiles(f_row, f_um, f_lp, f_dm, f_dp)
    h = tiles(h_row, h_um, h_lp, h_dm, h_dp)

    def swap(k, src, dst_from_left, dst_from_right):
        return (
            remote(src, dst_from_left, tile_s.at[k, 0], tile_r.at[k, 0], right),
            remote(src, dst_from_right, tile_s.at[k, 1], tile_r.at[k, 1], left),
        )

    def node(x, y):
        return [(x["d"], y["d"]), (x["u"], y["lp"]), (x["l"], y["um"])]

    def edge_um(x, y):
        return [(x["dm"], y["um"]), (x["um"], y["d"])]

    def edge_lp(x, y):
        return [(x["dp"], y["lp"]), (x["lp"], y["d"])]

    def edge_l(x, y):
        return [(x["d"], y["l"]), (x["l"], y["dm"])]

    def edge_u(x, y):
        return [(x["d"], y["u"]), (x["u"], y["dp"])]

    product(node(a, a), to_factor(f["d"], k_d, True))
    sent_f = swap(0, f["d"], f_dm, f_dp)
    product(edge_um(a, a), to_factor(f["um"], keep_um, False))
    product(edge_lp(a, a), to_factor(f["lp"], keep_lp, False))
    product(node(a, f), to_next(b["d"], k_d, BF))
    sent_b = swap(1, b["d"], b["dm"], b["dp"])
    product(edge_l(a, a), to_factor(f["l"], k_l, False))
    product(edge_u(a, a), to_factor(f["u"], k_u, False))
    product(edge_um(a, f), to_next(b["um"], keep_um, BF))
    product(edge_lp(a, f), to_next(b["lp"], keep_lp, BF))

    sent_f[0].wait_recv()
    product(edge_l(a, f), to_next(b["l"], k_l, BF))
    sent_f[1].wait_recv()
    product(edge_u(a, f), to_next(b["u"], k_u, BF))

    product(node(b, b), to_factor(h["d"], k_d, True))
    sent_h = swap(2, h["d"], h_dm, h_dp)
    sent_b[0].wait_recv()
    product(edge_um(b, b), to_factor(h["um"], keep_um, False))
    product(edge_l(b, b), to_factor(h["l"], k_l, False))
    sent_b[1].wait_recv()
    product(edge_lp(b, b), to_factor(h["lp"], keep_lp, False))
    product(edge_u(b, b), to_factor(h["u"], k_u, False))
    product(node(b, h), to_next(out_ref.at[:, pl.ds(T, T)], k_d, F32))
    sent_h[0].wait_recv()
    product(edge_l(b, h), to_next(out_ref.at[:, pl.ds(0, T)], k_l, F32))
    sent_h[1].wait_recv()
    product(edge_u(b, h), to_next(out_ref.at[:, pl.ds(2 * T, T)], k_u, F32))

    for copy in arrive.values():
        copy.wait_send()
    for copy in halo.values():
        copy.wait_send()
    for copy in (*pending, *sent_f, *sent_b, *sent_h):
        copy.wait_send()


def on_device(assembled, dest_group, block_mask):
    tile = pltpu.VMEM((T, T), BF)
    row = pltpu.VMEM((T, 3 * T), BF)
    pair = pltpu.VMEM((T, 2 * T), BF)
    dma = pltpu.SemaphoreType.DMA
    return pl.pallas_call(
        kernel,
        out_shape=jax.ShapeDtypeStruct((T, 3 * T), F32),
        in_specs=[
            pl.BlockSpec(memory_space=pltpu.VMEM),
            pl.BlockSpec(memory_space=pltpu.VMEM),
            pl.BlockSpec(memory_space=pltpu.VMEM),
        ],
        out_specs=pl.BlockSpec(memory_space=pltpu.VMEM),
        scratch_shapes=[
            pltpu.VMEM((4, CHUNK, 3 * T), BF), row,
            pltpu.VMEM((CB, 128), F32), pltpu.VMEM((CB, 128), F32), pltpu.VMEM((CB, 128), F32),
            row, tile, tile,
            row, pair, pair, row, tile, tile, tile, tile,
            row, pair, pair, row, tile, tile, tile, tile,
            dma((4, 2)), dma((4, 2)), dma((2, 4, 2)), dma((2, 4, 2)), dma((3, 2)), dma((3, 2)), dma((2,)), dma((2,)),
        ],
        compiler_params=pltpu.CompilerParams(
            collective_id=0, has_side_effects=True, vmem_limit_bytes=56 * 2**20
        ),
        cost_estimate=pl.CostEstimate(flops=40 * 2 * T**3, bytes_accessed=9 * T * T * 2, transcendentals=0),
        name="sign_steps",
    )(assembled, dest_group, block_mask)


def solution(mesh):
    spec = P(("grp", "pan"), None)
    return jax.shard_map(on_device, mesh=mesh, in_specs=(spec, spec, spec), out_specs=spec, check_vma=False)
```

```python
import jax
import jax.numpy as jnp
from jax import lax
from jax.experimental import pallas as pl
from jax.experimental.pallas import tpu as pltpu
from jax.sharding import PartitionSpec as P

MESH = pl.DeviceIdType.MESH
ATOM = 64
CB = 8
T = ATOM * CB
CHUNK = 2 * ATOM
H = 256
BF = jnp.bfloat16
F32 = jnp.float32


def kernel(
    x_ref, dest_ref, mask_ref, out_ref,
    for_far, for_sib, transit, land, mine, mask_l, mask_r, keep, keep_hl, keep_hr,
    a_row, a_hl, a_hr, f_row, f_um, f_lp, f_dm, f_dp,
    b_row, b_hl, b_hr, h_row, h_um, h_lp, h_dm, h_dp,
    sib_s, sib_r, hop_s, hop_r, far_s, far_r, halo_s, halo_r, extra_s, tile_s, tile_r, m_s, m_r,
):
    g = lax.axis_index("grp")
    p = lax.axis_index("pan")
    n = lax.axis_size("pan")
    core = lax.rem(g, 2)
    y_hi = g // 2
    z = lax.rem(p, 4)
    sib = g + 1 - 2 * core
    far = lax.rem(g + 2, 4)
    far_sib = lax.rem(sib + 2, 4)
    wraps = jnp.logical_or(z == 0, z == 3)

    def across(pan):
        return pan + 4 - 8 * lax.rem(pan // 4, 2)

    before, after = lax.rem(p + n - 1, n), lax.rem(p + 1, n)
    inner = across(p)
    left, right = (g, before), (g, after)
    outer_to = (far, inner)
    inner_to = ((g, inner), (sib, inner))
    chunk_of = (g, sib, far, far_sib)

    barrier = pltpu.get_barrier_semaphore()

    def greet(other):
        pl.semaphore_signal(barrier, inc=1, device_id=other, device_id_type=MESH)

    for other in ((sib, p), outer_to, *inner_to, left, right):
        greet(other)

    @pl.when(z == 0)
    def _():
        for who in (g, sib):
            greet((who, across(before)))

    @pl.when(z == 3)
    def _():
        for who in (g, sib):
            greet((who, across(after)))

    def one_hot(rows, cols, of_row, of_col):
        row = of_row(lax.broadcasted_iota(jnp.int32, (rows, cols), 0))
        return (row == of_col(lax.broadcasted_iota(jnp.int32, (rows, cols), 1))).astype(F32)

    eye = one_hot(CB, CB, lambda v: v, lambda v: v)
    lane = lax.broadcasted_iota(jnp.int32, (1, CB), 1)
    key_row = (dest_ref[...] * CB + lane).astype(F32)
    key_col = jnp.sum(eye * key_row, axis=1, keepdims=True)
    rank = jnp.sum((key_col < key_row).astype(F32), axis=0, keepdims=True)
    spread = one_hot(CB, T, lambda v: v, lambda v: v // ATOM)
    slot = jnp.sum(spread * jnp.sum(eye * rank, axis=1, keepdims=True), axis=0, keepdims=True)
    slot = slot * ATOM + (lax.broadcasted_iota(jnp.int32, (1, T), 1) % ATOM).astype(F32)

    def rows_for(group):
        want = (group * CHUNK + lax.broadcasted_iota(jnp.int32, (CHUNK, T), 0)).astype(F32)
        pick = (want == slot).astype(BF)
        return jnp.dot(pick, x_ref[...], preferred_element_type=F32).astype(BF)

    def rows_at(k, t, count):
        return pl.ds(pl.multiple_of(chunk_of[k] * CHUNK + t * ATOM, ATOM), count)

    for_far[0] = rows_for(far)
    for_far[1] = rows_for(far_sib)
    for_sib[...] = rows_for(sib)
    land[rows_at(0, 0, CHUNK), :] = rows_for(g)
    mine[...] = jnp.zeros_like(mine)
    mine[:, : 3 * CB] = mask_ref[...].astype(F32)

    @pl.when(wraps)
    def _():
        pl.semaphore_wait(barrier, 8)

    @pl.when(jnp.logical_not(wraps))
    def _():
        pl.semaphore_wait(barrier, 6)

    def describe(src, dst, ss, rs, to):
        return pltpu.make_async_remote_copy(
            src_ref=src, dst_ref=dst, send_sem=ss, recv_sem=rs, device_id=to, device_id_type=MESH
        )

    pending = []

    def remote(*what):
        copy = describe(*what)
        copy.start()
        pending.append((None, copy))
        return copy

    def remote_when(cond, *what):
        copy = describe(*what)

        @pl.when(cond)
        def _():
            copy.start()

        pending.append((cond, copy))
        return copy

    hop = {}
    for t in range(2):
        for k in range(2):
            rows = pl.ds(t * ATOM, ATOM)
            hop[k, t] = remote(for_far.at[k, rows], transit.at[k, rows], hop_s.at[k, t], hop_r.at[k, t], outer_to)
    here = rows_at(0, 0, CHUNK)
    from_sib = remote(for_sib, land.at[here], sib_s, sib_r, (sib, p))
    mask_in = (
        remote(mine, mask_l, m_s.at[0], m_r.at[0], right),
        remote(mine, mask_r, m_s.at[1], m_r.at[1], left),
    )
    halo = []
    right_cols, left_cols = pl.ds(T, 2 * T), pl.ds(0, 2 * T)

    def spread_out(k, t, count):
        rows = rows_at(k, t, count)
        to_right = (land.at[rows, right_cols], a_hl.at[rows], halo_s.at[0, k, t], halo_r.at[0, k, t], right)
        to_left = (land.at[rows, left_cols], a_hr.at[rows], halo_s.at[1, k, t], halo_r.at[1, k, t], left)
        if k < 2:
            halo.append(remote(*to_right))
            halo.append(remote(*to_left))
        else:
            halo.append(remote_when(z != 3, *to_right))
            halo.append(remote_when(z != 0, *to_left))

    arrive = {}

    def forward(k, t):
        hop[k, t].wait_recv()
        rows = pl.ds(t * ATOM, ATOM)
        at = pl.ds(pl.multiple_of(far * CHUNK + t * ATOM, ATOM), ATOM)
        who = (g, sib)[k]
        arrive[k, t] = remote(transit.at[k, rows], land.at[at], far_s.at[k, t], far_r.at[k, t], inner_to[k])
        remote_when(
            z == 3, transit.at[k, rows, right_cols], a_hl.at[at], extra_s.at[0, k, t], halo_r.at[0, 2 + k, t],
            (who, lax.rem(inner + 1, n)),
        )
        remote_when(
            z == 0, transit.at[k, rows, left_cols], a_hr.at[at], extra_s.at[1, k, t], halo_r.at[1, 2 + k, t],
            (who, lax.rem(inner + n - 1, n)),
        )

    def settle(k, t):
        arrive[k, t].wait_recv()
        spread_out(2 + k, t, ATOM)

    def expand(block, dst):
        rows = block.shape[0] * ATOM
        cols = block.shape[1] * ATOM
        up = one_hot(rows, CB, lambda v: v // ATOM, lambda v: v).astype(BF)
        over = one_hot(block.shape[1], cols, lambda v: v, lambda v: v // ATOM).astype(BF)
        tall = jnp.dot(up, block.astype(BF), preferred_element_type=F32)
        dst[...] = jnp.dot(tall.astype(BF), over, preferred_element_type=F32).astype(BF)

    spread_out(0, 0, CHUNK)
    from_sib.wait_recv()
    spread_out(1, 0, CHUNK)
    expand(mine[:, : 3 * CB], keep)
    forward(0, 0)
    forward(1, 0)
    settle(0, 0)
    forward(0, 1)
    settle(1, 0)
    forward(1, 1)
    mask_in[0].wait_recv()
    mask_in[1].wait_recv()
    expand(mask_l[:, CB : 3 * CB], keep_hl)
    expand(mask_r[:, : 2 * CB], keep_hr)
    settle(0, 1)
    settle(1, 1)
    a_row[...] = land[...] * keep[...]
    for copy in halo:
        copy.wait_recv()
    a_hl[...] = a_hl[...] * keep_hl[...]
    a_hr[...] = a_hr[...] * keep_hr[...]
    keep_um = keep_hl.at[:, pl.ds(T, T)]
    keep_lp = keep_hr.at[:, pl.ds(0, T)]

    def tile_of(ref, k):
        return ref.at[:, pl.ds(k * T, T)]

    def product(pairs, finish):
        for i in range(T // H):
            for j in range(T // H):
                acc = None
                for a, b in pairs:
                    part = jnp.dot(
                        a[i * H : (i + 1) * H, :], b[:, j * H : (j + 1) * H], preferred_element_type=F32
                    )
                    acc = part if acc is None else acc + part
                finish(i, j, acc)

    def to_factor(dst, mask, diagonal):
        def finish(i, j, acc):
            at = (slice(i * H, (i + 1) * H), slice(j * H, (j + 1) * H))
            value = acc * mask[at].astype(F32) * (-1.0 / (3.0 * T))
            if diagonal and i == j:
                same = lax.broadcasted_iota(jnp.int32, (H, H), 0) == lax.broadcasted_iota(jnp.int32, (H, H), 1)
                value = jnp.where(same, 3.0 + value, value)
            dst[at] = value.astype(BF)

        return finish

    def to_next(dst, mask, dtype):
        def finish(i, j, acc):
            at = (slice(i * H, (i + 1) * H), slice(j * H, (j + 1) * H))
            dst[at] = (0.5 * acc * mask[at].astype(F32)).astype(dtype)

        return finish

    k_l, k_d, k_u = (tile_of(keep, k) for k in range(3))

    def tiles(row, um_ref, lp_ref, dm_ref, dp_ref):
        return dict(l=tile_of(row, 0), d=tile_of(row, 1), u=tile_of(row, 2), um=um_ref, lp=lp_ref, dm=dm_ref, dp=dp_ref)

    a = tiles(a_row, tile_of(a_hl, 1), tile_of(a_hr, 0), tile_of(a_hl, 0), tile_of(a_hr, 1))
    b = tiles(b_row, tile_of(b_hl, 1), tile_of(b_hr, 0), tile_of(b_hl, 0), tile_of(b_hr, 1))
    f = tiles(f_row, f_um, f_lp, f_dm, f_dp)
    h = tiles(h_row, h_um, h_lp, h_dm, h_dp)

    def swap(k, src, dst_from_left, dst_from_right):
        return (
            remote(src, dst_from_left, tile_s.at[k, 0], tile_r.at[k, 0], right),
            remote(src, dst_from_right, tile_s.at[k, 1], tile_r.at[k, 1], left),
        )

    def node(x, y):
        return [(x["d"], y["d"]), (x["u"], y["lp"]), (x["l"], y["um"])]

    def edge_um(x, y):
        return [(x["dm"], y["um"]), (x["um"], y["d"])]

    def edge_lp(x, y):
        return [(x["dp"], y["lp"]), (x["lp"], y["d"])]

    def edge_l(x, y):
        return [(x["d"], y["l"]), (x["l"], y["dm"])]

    def edge_u(x, y):
        return [(x["d"], y["u"]), (x["u"], y["dp"])]

    product(node(a, a), to_factor(f["d"], k_d, True))
    sent_f = swap(0, f["d"], f_dm, f_dp)
    product(edge_um(a, a), to_factor(f["um"], keep_um, False))
    product(edge_lp(a, a), to_factor(f["lp"], keep_lp, False))
    product(node(a, f), to_next(b["d"], k_d, BF))
    sent_b = swap(1, b["d"], b["dm"], b["dp"])
    product(edge_l(a, a), to_factor(f["l"], k_l, False))
    product(edge_u(a, a), to_factor(f["u"], k_u, False))
    product(edge_um(a, f), to_next(b["um"], keep_um, BF))
    product(edge_lp(a, f), to_next(b["lp"], keep_lp, BF))

    sent_f[0].wait_recv()
    product(edge_l(a, f), to_next(b["l"], k_l, BF))
    sent_f[1].wait_recv()
    product(edge_u(a, f), to_next(b["u"], k_u, BF))

    product(node(b, b), to_factor(h["d"], k_d, True))
    sent_h = swap(2, h["d"], h_dm, h_dp)
    sent_b[0].wait_recv()
    product(edge_um(b, b), to_factor(h["um"], keep_um, False))
    product(edge_l(b, b), to_factor(h["l"], k_l, False))
    sent_b[1].wait_recv()
    product(edge_lp(b, b), to_factor(h["lp"], keep_lp, False))
    product(edge_u(b, b), to_factor(h["u"], k_u, False))
    product(node(b, h), to_next(out_ref.at[:, pl.ds(T, T)], k_d, F32))
    sent_h[0].wait_recv()
    product(edge_l(b, h), to_next(out_ref.at[:, pl.ds(0, T)], k_l, F32))
    sent_h[1].wait_recv()
    product(edge_u(b, h), to_next(out_ref.at[:, pl.ds(2 * T, T)], k_u, F32))

    for cond, copy in pending:
        if cond is None:
            copy.wait_send()
        else:
            pl.when(cond)(copy.wait_send)


def on_device(assembled, dest_group, block_mask):
    tile = pltpu.VMEM((T, T), BF)
    row = pltpu.VMEM((T, 3 * T), BF)
    pair = pltpu.VMEM((T, 2 * T), BF)
    dma = pltpu.SemaphoreType.DMA
    return pl.pallas_call(
        kernel,
        out_shape=jax.ShapeDtypeStruct((T, 3 * T), F32),
        in_specs=[
            pl.BlockSpec(memory_space=pltpu.VMEM),
            pl.BlockSpec(memory_space=pltpu.VMEM),
            pl.BlockSpec(memory_space=pltpu.VMEM),
        ],
        out_specs=pl.BlockSpec(memory_space=pltpu.VMEM),
        scratch_shapes=[
            pltpu.VMEM((2, CHUNK, 3 * T), BF), pltpu.VMEM((CHUNK, 3 * T), BF), pltpu.VMEM((2, CHUNK, 3 * T), BF), row,
            pltpu.VMEM((CB, 128), F32), pltpu.VMEM((CB, 128), F32), pltpu.VMEM((CB, 128), F32),
            row, pair, pair,
            row, pair, pair, row, tile, tile, tile, tile,
            row, pair, pair, row, tile, tile, tile, tile,
            dma, dma, dma((2, 2)), dma((2, 2)), dma((2, 2)), dma((2, 2)),
            dma((2, 4, 2)), dma((2, 4, 2)), dma((2, 2, 2)), dma((3, 2)), dma((3, 2)), dma((2,)), dma((2,)),
        ],
        compiler_params=pltpu.CompilerParams(
            collective_id=0, has_side_effects=True, vmem_limit_bytes=56 * 2**20
        ),
        cost_estimate=pl.CostEstimate(flops=40 * 2 * T**3, bytes_accessed=9 * T * T * 2, transcendentals=0),
        name="sign_steps",
    )(assembled, dest_group, block_mask)


def solution(mesh):
    spec = P(("grp", "pan"), None)
    return jax.shard_map(on_device, mesh=mesh, in_specs=(spec, spec, spec), out_specs=spec, check_vma=False)
```

```python
import functools

import jax
import jax.numpy as jnp
from jax import lax
from jax.experimental import pallas as pl
from jax.experimental.pallas import tpu as pltpu
from jax.sharding import PartitionSpec as P

MESH = pl.DeviceIdType.MESH
ATOM = 64
CB = 8
T = ATOM * CB
CHUNK = 2 * ATOM
H = 256
CUTS = (0, 64, 96, 128)
PIECES = len(CUTS) - 1
BF = jnp.bfloat16
F32 = jnp.float32


def kernel(
    x_ref, dest_ref, mask_ref, out_ref,
    for_far, for_sib, transit, land, mine, mask_l, mask_r, keep, keep_hl, keep_hr,
    a_row, a_hl, a_hr, f_row, f_um, f_lp, f_dm, f_dp,
    b_row, b_hl, b_hr, h_row, h_um, h_lp, h_dm, h_dp,
    sib_s, sib_r, hop_s, hop_r, far_s, far_r, halo_s, halo_r, extra_s, tile_s, tile_r, m_s, m_r,
):
    g = lax.axis_index("grp")
    p = lax.axis_index("pan")
    n = lax.axis_size("pan")
    core = lax.rem(g, 2)
    y_hi = g // 2
    z = lax.rem(p, 4)
    sib = g + 1 - 2 * core
    far = lax.rem(g + 2, 4)
    other_hi = 2 - 2 * y_hi
    wraps = jnp.logical_or(z == 0, z == 3)

    def across(pan):
        return pan + 4 - 8 * lax.rem(pan // 4, 2)

    before, after = lax.rem(p + n - 1, n), lax.rem(p + 1, n)
    inner = across(p)
    left, right = (g, before), (g, after)
    outer_to = (far, inner)
    inner_to = ((g, inner), (sib, inner))

    barrier = pltpu.get_barrier_semaphore()

    def greet(other):
        pl.semaphore_signal(barrier, inc=1, device_id=other, device_id_type=MESH)

    for other in ((sib, p), outer_to, *inner_to, left, right):
        greet(other)

    @pl.when(z == 0)
    def _():
        for who in (g, sib):
            greet((who, across(before)))

    @pl.when(z == 3)
    def _():
        for who in (g, sib):
            greet((who, across(after)))

    def one_hot(rows, cols, of_row, of_col):
        row = of_row(lax.broadcasted_iota(jnp.int32, (rows, cols), 0))
        return (row == of_col(lax.broadcasted_iota(jnp.int32, (rows, cols), 1))).astype(F32)

    eye = one_hot(CB, CB, lambda v: v, lambda v: v)
    lane = lax.broadcasted_iota(jnp.int32, (1, CB), 1)
    key_row = (dest_ref[...] * CB + lane).astype(F32)
    key_col = jnp.sum(eye * key_row, axis=1, keepdims=True)
    rank = jnp.sum((key_col < key_row).astype(F32), axis=0, keepdims=True)
    spread = one_hot(CB, T, lambda v: v, lambda v: v // ATOM)
    goal = jnp.sum(spread * jnp.sum(eye * rank, axis=1, keepdims=True), axis=0, keepdims=True)
    goal = goal * ATOM + (lax.broadcasted_iota(jnp.int32, (1, T), 1) % ATOM).astype(F32)

    def rows_for(group):
        want = (group * CHUNK + lax.broadcasted_iota(jnp.int32, (CHUNK, T), 0)).astype(F32)
        pick = (want == goal).astype(BF)
        return jnp.dot(pick, x_ref[...], preferred_element_type=F32).astype(BF)

    def rows_of(group, t=None):
        if t is None:
            return pl.ds(pl.multiple_of(group * CHUNK, CHUNK), CHUNK)
        return pl.ds(pl.multiple_of(group * CHUNK + CUTS[t], 16), CUTS[t + 1] - CUTS[t])

    sends = []

    def describe(src, dst, ss, rs, to):
        return pltpu.make_async_remote_copy(
            src_ref=src, dst_ref=dst, send_sem=ss, recv_sem=rs, device_id=to, device_id_type=MESH
        )

    def remote(*what):
        copy = describe(*what)
        copy.start()
        sends.append((None, lambda: copy))
        return copy

    def piece(t):
        return pl.ds(CUTS[t], CUTS[t + 1] - CUTS[t])

    def hop(d, t):
        return describe(for_far.at[d, piece(t)], transit.at[d, piece(t)], hop_s.at[d, t], hop_r.at[d, t], outer_to)

    for_far[0] = rows_for(other_hi)
    for_far[1] = rows_for(other_hi + 1)

    @pl.when(wraps)
    def _():
        pl.semaphore_wait(barrier, 8)

    @pl.when(jnp.logical_not(wraps))
    def _():
        pl.semaphore_wait(barrier, 6)

    def launch(t):
        for d in range(2):
            hop(d, t).start()
            sends.append((None, functools.partial(hop, d, t)))

    for t in range(PIECES):
        launch(t)
    mine[...] = jnp.zeros_like(mine)
    mine[:, : 3 * CB] = mask_ref[...].astype(F32)
    mask_in = (
        remote(mine, mask_l, m_s.at[0], m_r.at[0], right),
        remote(mine, mask_r, m_s.at[1], m_r.at[1], left),
    )
    for_sib[...] = rows_for(sib)
    from_sib = remote(for_sib, land.at[rows_of(g)], sib_s, sib_r, (sib, p))
    land[rows_of(g), :] = rows_for(g)

    right_cols, left_cols = pl.ds(T, 2 * T), pl.ds(0, 2 * T)
    slots = [rows_of(g), rows_of(sib)] + [rows_of(other_hi + c, t) for c in range(2) for t in range(PIECES)]

    def halo(side, slot):
        rows = slots[slot]
        if side == 0:
            return describe(land.at[rows, right_cols], a_hl.at[rows], halo_s.at[0, slot], halo_r.at[0, slot], right)
        return describe(land.at[rows, left_cols], a_hr.at[rows], halo_s.at[1, slot], halo_r.at[1, slot], left)

    def start_when(cond, copy):
        pl.when(cond)(copy.start)

    def onward(d, t):
        at = rows_of(far, t)
        return describe(transit.at[d, piece(t)], land.at[at], far_s.at[d, t], far_r.at[core, t], (y_hi * 2 + d, inner))

    def extra(side, d, t):
        at = rows_of(far, t)
        to = (y_hi * 2 + d, lax.rem(inner + (1 if side == 0 else n - 1), n))
        cols, dst = ((right_cols, a_hl), (left_cols, a_hr))[side]
        return describe(
            transit.at[d, piece(t), cols], dst.at[at], extra_s.at[side, d, t], halo_r.at[side, 2 + PIECES * core + t], to
        )

    def forward(d, t):
        hop(d, t).wait_recv()
        onward(d, t).start()
        start_when(z == 3, extra(0, d, t))
        start_when(z == 0, extra(1, d, t))

    def settle(c, t):
        slot = 2 + PIECES * c + t
        rows = slots[slot]
        describe(transit.at[0, piece(t)], land.at[rows], far_s.at[0, t], far_r.at[c, t], right).wait_recv()
        start_when(z != 3, halo(0, slot))
        start_when(z != 0, halo(1, slot))
        a_row[rows, :] = land[rows, :] * keep[rows, :]

    def expand(block, dst):
        rows = block.shape[0] * ATOM
        cols = block.shape[1] * ATOM
        up = one_hot(rows, CB, lambda v: v // ATOM, lambda v: v).astype(BF)
        over = one_hot(block.shape[1], cols, lambda v: v, lambda v: v // ATOM).astype(BF)
        tall = jnp.dot(up, block.astype(BF), preferred_element_type=F32)
        dst[...] = jnp.dot(tall.astype(BF), over, preferred_element_type=F32).astype(BF)

    def spread_near(slot):
        for side in range(2):
            halo(side, slot).start()

    spread_near(0)
    expand(mine[:, : 3 * CB], keep)
    from_sib.wait_recv()
    spread_near(1)
    mask_in[0].wait_recv()
    mask_in[1].wait_recv()
    expand(mask_l[:, CB : 3 * CB], keep_hl)
    expand(mask_r[:, : 2 * CB], keep_hr)
    for slot in range(2):
        a_row[slots[slot], :] = land[slots[slot], :] * keep[slots[slot], :]

    for t in range(PIECES):
        for k in range(2):
            forward(k, t)
            if t:
                settle(k, t - 1)
    for k in range(2):
        settle(k, PIECES - 1)

    for d in range(2):
        for t in range(PIECES):
            sends.append((None, functools.partial(onward, d, t)))
            sends.append((z == 3, functools.partial(extra, 0, d, t)))
            sends.append((z == 0, functools.partial(extra, 1, d, t)))
    for slot in [0, 1] + [2 + PIECES * c + t for t in range(PIECES) for c in range(2)]:
        for side, (dst, mask) in enumerate(((a_hl, keep_hl), (a_hr, keep_hr))):
            halo(side, slot).wait_recv()
            rows = slots[slot]
            dst[rows, :] = dst[rows, :] * mask[rows, :]
            away = None if slot < 2 else (z != 3, z != 0)[side]
            sends.append((away, functools.partial(halo, side, slot)))
    keep_um = keep_hl.at[:, pl.ds(T, T)]
    keep_lp = keep_hr.at[:, pl.ds(0, T)]

    def tile_of(ref, k):
        return ref.at[:, pl.ds(k * T, T)]

    def product(pairs, finish, after=None):
        for i in range(T // H):
            for j in range(T // H):
                acc = None
                for a, b in pairs:
                    part = jnp.dot(
                        a[i * H : (i + 1) * H, :], b[:, j * H : (j + 1) * H], preferred_element_type=F32
                    )
                    acc = part if acc is None else acc + part
                finish(i, j, acc)
            if after is not None:
                after(i)

    def to_factor(dst, mask, diagonal):
        def finish(i, j, acc):
            at = (slice(i * H, (i + 1) * H), slice(j * H, (j + 1) * H))
            value = acc * mask[at].astype(F32) * (-1.0 / (3.0 * T))
            if diagonal and i == j:
                same = lax.broadcasted_iota(jnp.int32, (H, H), 0) == lax.broadcasted_iota(jnp.int32, (H, H), 1)
                value = jnp.where(same, 3.0 + value, value)
            dst[at] = value.astype(BF)

        return finish

    def to_next(dst, mask, dtype):
        def finish(i, j, acc):
            at = (slice(i * H, (i + 1) * H), slice(j * H, (j + 1) * H))
            dst[at] = (0.5 * acc * mask[at].astype(F32)).astype(dtype)

        return finish

    k_l, k_d, k_u = (tile_of(keep, k) for k in range(3))

    def tiles(row, um_ref, lp_ref, dm_ref, dp_ref):
        return dict(l=tile_of(row, 0), d=tile_of(row, 1), u=tile_of(row, 2), um=um_ref, lp=lp_ref, dm=dm_ref, dp=dp_ref)

    a = tiles(a_row, tile_of(a_hl, 1), tile_of(a_hr, 0), tile_of(a_hl, 0), tile_of(a_hr, 1))
    b = tiles(b_row, tile_of(b_hl, 1), tile_of(b_hr, 0), tile_of(b_hl, 0), tile_of(b_hr, 1))
    f = tiles(f_row, f_um, f_lp, f_dm, f_dp)
    h = tiles(h_row, h_um, h_lp, h_dm, h_dp)

    def sender(k, src, from_left, from_right):
        def swap(side, i):
            half = pl.ds(i * H, H)
            dst, to = ((from_left, right), (from_right, left))[side]
            return describe(src.at[half], dst.at[half], tile_s.at[k, side, i], tile_r.at[k, side, i], to)

        def after(i):
            for side in range(2):
                swap(side, i).start()
                sends.append((None, functools.partial(swap, side, i)))

        def wait(side, i):
            swap(side, i).wait_recv()

        return after, wait

    def node(x, y):
        return [(x["d"], y["d"]), (x["u"], y["lp"]), (x["l"], y["um"])]

    def edge_um(x, y):
        return [(x["dm"], y["um"]), (x["um"], y["d"])]

    def edge_lp(x, y):
        return [(x["dp"], y["lp"]), (x["lp"], y["d"])]

    def edge_l(x, y):
        return [(x["d"], y["l"]), (x["l"], y["dm"])]

    def edge_u(x, y):
        return [(x["d"], y["u"]), (x["u"], y["dp"])]

    send_f, wait_f = sender(0, f["d"], f_dm, f_dp)
    send_b, wait_b = sender(1, b["d"], b["dm"], b["dp"])
    send_h, wait_h = sender(2, h["d"], h_dm, h_dp)

    product(node(a, a), to_factor(f["d"], k_d, True), send_f)
    product(edge_um(a, a), to_factor(f["um"], keep_um, False))
    product(edge_lp(a, a), to_factor(f["lp"], keep_lp, False))
    product(node(a, f), to_next(b["d"], k_d, BF), send_b)
    product(edge_l(a, a), to_factor(f["l"], k_l, False))
    product(edge_u(a, a), to_factor(f["u"], k_u, False))
    product(edge_um(a, f), to_next(b["um"], keep_um, BF))
    product(edge_lp(a, f), to_next(b["lp"], keep_lp, BF))

    wait_f(0, 0)
    wait_f(0, 1)
    product(edge_l(a, f), to_next(b["l"], k_l, BF))
    wait_f(1, 0)
    wait_f(1, 1)
    product(edge_u(a, f), to_next(b["u"], k_u, BF))

    product(node(b, b), to_factor(h["d"], k_d, True), send_h)
    wait_b(0, 0)
    wait_b(0, 1)
    product(edge_um(b, b), to_factor(h["um"], keep_um, False))
    product(edge_l(b, b), to_factor(h["l"], k_l, False))
    wait_b(1, 0)
    wait_b(1, 1)
    product(edge_lp(b, b), to_factor(h["lp"], keep_lp, False))
    product(edge_u(b, b), to_factor(h["u"], k_u, False))
    out_l, out_d, out_u = (tile_of(out_ref, k) for k in range(3))
    product(node(b, h), to_next(out_d, k_d, F32))

    def keep_sum(dst):
        def finish(i, j, acc):
            dst[i * H : (i + 1) * H, j * H : (j + 1) * H] = acc

        return finish

    def add_half(dst, x, y, q, mask):
        part = pl.ds(q * H, H)

        def finish(i, j, acc):
            at = (slice(i * H, (i + 1) * H), slice(j * H, (j + 1) * H))
            total = dst[at] + acc
            dst[at] = total if mask is None else 0.5 * total * mask[at].astype(F32)

        product([(x.at[:, part], y.at[part, :])], finish)

    product([(b["d"], h["l"])], keep_sum(out_l))
    product([(b["d"], h["u"])], keep_sum(out_u))
    for q in range(2):
        wait_h(0, q)
        add_half(out_l, b["l"], h_dm, q, k_l if q else None)
        wait_h(1, q)
        add_half(out_u, b["u"], h_dp, q, k_u if q else None)

    for cond, make in sends:
        if cond is None:
            make().wait_send()
        else:
            pl.when(cond)(make().wait_send)


def on_device(assembled, dest_group, block_mask):
    tile = pltpu.VMEM((T, T), BF)
    row = pltpu.VMEM((T, 3 * T), BF)
    pair = pltpu.VMEM((T, 2 * T), BF)
    dma = pltpu.SemaphoreType.DMA
    return pl.pallas_call(
        kernel,
        out_shape=jax.ShapeDtypeStruct((T, 3 * T), F32),
        in_specs=[
            pl.BlockSpec(memory_space=pltpu.VMEM),
            pl.BlockSpec(memory_space=pltpu.VMEM),
            pl.BlockSpec(memory_space=pltpu.VMEM),
        ],
        out_specs=pl.BlockSpec(memory_space=pltpu.VMEM),
        scratch_shapes=[
            pltpu.VMEM((2, CHUNK, 3 * T), BF), pltpu.VMEM((CHUNK, 3 * T), BF), pltpu.VMEM((2, CHUNK, 3 * T), BF), row,
            pltpu.VMEM((CB, 128), F32), pltpu.VMEM((CB, 128), F32), pltpu.VMEM((CB, 128), F32),
            row, pair, pair,
            row, pair, pair, row, tile, tile, tile, tile,
            row, pair, pair, row, tile, tile, tile, tile,
            dma, dma, dma((2, PIECES)), dma((2, PIECES)), dma((2, PIECES)), dma((2, PIECES)),
            dma((2, 2 + 2 * PIECES)), dma((2, 2 + 2 * PIECES)), dma((2, 2, PIECES)), dma((3, 2, 2)), dma((3, 2, 2)), dma((2,)), dma((2,)),
        ],
        compiler_params=pltpu.CompilerParams(
            collective_id=0, has_side_effects=True, vmem_limit_bytes=36 * 2**20
        ),
        cost_estimate=pl.CostEstimate(flops=40 * 2 * T**3, bytes_accessed=9 * T * T * 2, transcendentals=0),
        name="sign_steps",
    )(assembled, dest_group, block_mask)


def solution(mesh):
    spec = P(("grp", "pan"), None)
    return jax.shard_map(on_device, mesh=mesh, in_specs=(spec, spec, spec), out_specs=spec, check_vma=False)
```

```python
import functools

import jax
import jax.numpy as jnp
from jax import lax
from jax.experimental import pallas as pl
from jax.experimental.pallas import tpu as pltpu
from jax.sharding import PartitionSpec as P

MESH = pl.DeviceIdType.MESH
ATOM = 64
CB = 8
T = ATOM * CB
CHUNK = 2 * ATOM
H = 256
CUTS = (0, 64, 96, 128)
PIECES = len(CUTS) - 1
BF = jnp.bfloat16
F32 = jnp.float32


def kernel(
    x_ref, dest_ref, mask_ref, out_ref,
    for_far, for_sib, transit, land, mine, mask_l, mask_r, keep, keep_hl, keep_hr,
    a_row, a_hl, a_hr, f_row, f_um, f_lp, f_dm, f_dp,
    b_row, b_hl, b_hr, h_row, h_um, h_lp, h_dm, h_dp,
    sib_s, sib_r, hop_s, hop_r, far_s, far_r, halo_s, halo_r, extra_s, tile_s, tile_r, m_s, m_r,
):
    g = lax.axis_index("grp")
    p = lax.axis_index("pan")
    n = lax.axis_size("pan")
    core = lax.rem(g, 2)
    y_hi = g // 2
    z = lax.rem(p, 4)
    sib = g + 1 - 2 * core
    far = lax.rem(g + 2, 4)
    other_hi = 2 - 2 * y_hi
    wraps = jnp.logical_or(z == 0, z == 3)

    def across(pan):
        return pan + 4 - 8 * lax.rem(pan // 4, 2)

    before, after = lax.rem(p + n - 1, n), lax.rem(p + 1, n)
    inner = across(p)
    left, right = (g, before), (g, after)
    outer_to = (far, inner)
    inner_to = ((g, inner), (sib, inner))

    barrier = pltpu.get_barrier_semaphore()

    def greet(other):
        pl.semaphore_signal(barrier, inc=1, device_id=other, device_id_type=MESH)

    for other in ((sib, p), outer_to, *inner_to, left, right):
        greet(other)

    @pl.when(z == 0)
    def _():
        for who in (g, sib):
            greet((who, across(before)))

    @pl.when(z == 3)
    def _():
        for who in (g, sib):
            greet((who, across(after)))

    def one_hot(rows, cols, of_row, of_col):
        row = of_row(lax.broadcasted_iota(jnp.int32, (rows, cols), 0))
        return (row == of_col(lax.broadcasted_iota(jnp.int32, (rows, cols), 1))).astype(F32)

    eye = one_hot(CB, CB, lambda v: v, lambda v: v)
    lane = lax.broadcasted_iota(jnp.int32, (1, CB), 1)
    key_row = (dest_ref[...] * CB + lane).astype(F32)
    key_col = jnp.sum(eye * key_row, axis=1, keepdims=True)
    rank = jnp.sum((key_col < key_row).astype(F32), axis=0, keepdims=True)
    spread = one_hot(CB, T, lambda v: v, lambda v: v // ATOM)
    goal = jnp.sum(spread * jnp.sum(eye * rank, axis=1, keepdims=True), axis=0, keepdims=True)
    goal = goal * ATOM + (lax.broadcasted_iota(jnp.int32, (1, T), 1) % ATOM).astype(F32)

    def rows_for(group):
        want = (group * CHUNK + lax.broadcasted_iota(jnp.int32, (CHUNK, T), 0)).astype(F32)
        pick = (want == goal).astype(BF)
        return jnp.dot(pick, x_ref[...], preferred_element_type=F32).astype(BF)

    def rows_of(group, t=None):
        if t is None:
            return pl.ds(pl.multiple_of(group * CHUNK, CHUNK), CHUNK)
        return pl.ds(pl.multiple_of(group * CHUNK + CUTS[t], 16), CUTS[t + 1] - CUTS[t])

    sends = []

    def describe(src, dst, ss, rs, to):
        return pltpu.make_async_remote_copy(
            src_ref=src, dst_ref=dst, send_sem=ss, recv_sem=rs, device_id=to, device_id_type=MESH
        )

    def remote(*what):
        copy = describe(*what)
        copy.start()
        sends.append((None, lambda: copy))
        return copy

    def piece(t):
        return pl.ds(CUTS[t], CUTS[t + 1] - CUTS[t])

    def hop(d, t):
        return describe(for_far.at[d, piece(t)], transit.at[d, piece(t)], hop_s.at[d, t], hop_r.at[d, t], outer_to)

    for_far[0] = rows_for(other_hi)
    for_far[1] = rows_for(other_hi + 1)

    @pl.when(wraps)
    def _():
        pl.semaphore_wait(barrier, 8)

    @pl.when(jnp.logical_not(wraps))
    def _():
        pl.semaphore_wait(barrier, 6)

    turns = (core, 1 - core)

    def launch(t):
        for d in turns:
            hop(d, t).start()
            sends.append((None, functools.partial(hop, d, t)))

    for t in range(PIECES):
        launch(t)
    mine[...] = jnp.zeros_like(mine)
    mine[:, : 3 * CB] = mask_ref[...].astype(F32)
    mask_in = (
        remote(mine, mask_l, m_s.at[0], m_r.at[0], right),
        remote(mine, mask_r, m_s.at[1], m_r.at[1], left),
    )
    for_sib[...] = rows_for(sib)
    from_sib = remote(for_sib, land.at[rows_of(g)], sib_s, sib_r, (sib, p))
    land[rows_of(g), :] = rows_for(g)

    right_cols, left_cols = pl.ds(T, 2 * T), pl.ds(0, 2 * T)
    slots = [rows_of(g), rows_of(sib)] + [rows_of(other_hi + c, t) for c in range(2) for t in range(PIECES)]

    def halo(side, slot, rows=None):
        rows = slots[slot] if rows is None else rows
        if side == 0:
            return describe(land.at[rows, right_cols], a_hl.at[rows], halo_s.at[0, slot], halo_r.at[0, slot], right)
        return describe(land.at[rows, left_cols], a_hr.at[rows], halo_s.at[1, slot], halo_r.at[1, slot], left)

    def start_when(cond, copy):
        pl.when(cond)(copy.start)

    def onward(d, t):
        at = rows_of(far, t)
        return describe(transit.at[d, piece(t)], land.at[at], far_s.at[d, t], far_r.at[core, t], (y_hi * 2 + d, inner))

    def extra(side, d, t):
        at = rows_of(far, t)
        to = (y_hi * 2 + d, lax.rem(inner + (1 if side == 0 else n - 1), n))
        cols, dst = ((right_cols, a_hl), (left_cols, a_hr))[side]
        return describe(
            transit.at[d, piece(t), cols], dst.at[at], extra_s.at[side, d, t], halo_r.at[side, 2 + PIECES * core + t], to
        )

    def forward(d, t):
        hop(d, t).wait_recv()
        onward(d, t).start()
        start_when(z == 3, extra(0, d, t))
        start_when(z == 0, extra(1, d, t))

    def settle(c, t):
        slot = 2 + PIECES * c + t
        rows = rows_of(other_hi + c, t)
        describe(transit.at[0, piece(t)], land.at[rows], far_s.at[0, t], far_r.at[c, t], right).wait_recv()
        start_when(z != 3, halo(0, slot, rows))
        start_when(z != 0, halo(1, slot, rows))
        a_row[rows, :] = land[rows, :] * keep[rows, :]

    def expand(block, dst):
        rows = block.shape[0] * ATOM
        cols = block.shape[1] * ATOM
        up = one_hot(rows, CB, lambda v: v // ATOM, lambda v: v).astype(BF)
        over = one_hot(block.shape[1], cols, lambda v: v, lambda v: v // ATOM).astype(BF)
        tall = jnp.dot(up, block.astype(BF), preferred_element_type=F32)
        dst[...] = jnp.dot(tall.astype(BF), over, preferred_element_type=F32).astype(BF)

    def spread_near(slot):
        for side in range(2):
            halo(side, slot).start()

    spread_near(0)
    expand(mine[:, : 3 * CB], keep)
    from_sib.wait_recv()
    spread_near(1)
    mask_in[0].wait_recv()
    mask_in[1].wait_recv()
    expand(mask_l[:, CB : 3 * CB], keep_hl)
    expand(mask_r[:, : 2 * CB], keep_hr)
    for slot in range(2):
        a_row[slots[slot], :] = land[slots[slot], :] * keep[slots[slot], :]

    for t in range(PIECES):
        for k in range(2):
            forward(turns[k], t)
            if t:
                settle(turns[k], t - 1)
    for k in range(2):
        settle(turns[k], PIECES - 1)

    for d in range(2):
        for t in range(PIECES):
            sends.append((None, functools.partial(onward, d, t)))
            sends.append((z == 3, functools.partial(extra, 0, d, t)))
            sends.append((z == 0, functools.partial(extra, 1, d, t)))
    for slot in [0, 1] + [2 + PIECES * c + t for t in range(PIECES) for c in range(2)]:
        for side, (dst, mask) in enumerate(((a_hl, keep_hl), (a_hr, keep_hr))):
            halo(side, slot).wait_recv()
            rows = slots[slot]
            dst[rows, :] = dst[rows, :] * mask[rows, :]
            away = None if slot < 2 else (z != 3, z != 0)[side]
            sends.append((away, functools.partial(halo, side, slot)))
    keep_um = keep_hl.at[:, pl.ds(T, T)]
    keep_lp = keep_hr.at[:, pl.ds(0, T)]

    def tile_of(ref, k):
        return ref.at[:, pl.ds(k * T, T)]

    def product(pairs, finish, after=None):
        for i in range(T // H):
            for j in range(T // H):
                acc = None
                for a, b in pairs:
                    part = jnp.dot(
                        a[i * H : (i + 1) * H, :], b[:, j * H : (j + 1) * H], preferred_element_type=F32
                    )
                    acc = part if acc is None else acc + part
                finish(i, j, acc)
            if after is not None:
                after(i)

    def to_factor(dst, mask, diagonal):
        def finish(i, j, acc):
            at = (slice(i * H, (i + 1) * H), slice(j * H, (j + 1) * H))
            value = acc * mask[at].astype(F32) * (-1.0 / (3.0 * T))
            if diagonal and i == j:
                same = lax.broadcasted_iota(jnp.int32, (H, H), 0) == lax.broadcasted_iota(jnp.int32, (H, H), 1)
                value = jnp.where(same, 3.0 + value, value)
            dst[at] = value.astype(BF)

        return finish

    def to_next(dst, mask, dtype):
        def finish(i, j, acc):
            at = (slice(i * H, (i + 1) * H), slice(j * H, (j + 1) * H))
            dst[at] = (0.5 * acc * mask[at].astype(F32)).astype(dtype)

        return finish

    k_l, k_d, k_u = (tile_of(keep, k) for k in range(3))

    def tiles(row, um_ref, lp_ref, dm_ref, dp_ref):
        return dict(l=tile_of(row, 0), d=tile_of(row, 1), u=tile_of(row, 2), um=um_ref, lp=lp_ref, dm=dm_ref, dp=dp_ref)

    a = tiles(a_row, tile_of(a_hl, 1), tile_of(a_hr, 0), tile_of(a_hl, 0), tile_of(a_hr, 1))
    b = tiles(b_row, tile_of(b_hl, 1), tile_of(b_hr, 0), tile_of(b_hl, 0), tile_of(b_hr, 1))
    f = tiles(f_row, f_um, f_lp, f_dm, f_dp)
    h = tiles(h_row, h_um, h_lp, h_dm, h_dp)

    def sender(k, src, from_left, from_right):
        def swap(side, i):
            half = pl.ds(i * H, H)
            dst, to = ((from_left, right), (from_right, left))[side]
            return describe(src.at[half], dst.at[half], tile_s.at[k, side, i], tile_r.at[k, side, i], to)

        def after(i):
            for side in range(2):
                swap(side, i).start()

        def wait(side, i):
            swap(side, i).wait_recv()

        def drain():
            for i in range(T // H):
                for side in range(2):
                    swap(side, i).wait_send()

        return after, wait, drain

    def node(x, y):
        return [(x["d"], y["d"]), (x["u"], y["lp"]), (x["l"], y["um"])]

    def edge_um(x, y):
        return [(x["dm"], y["um"]), (x["um"], y["d"])]

    def edge_lp(x, y):
        return [(x["dp"], y["lp"]), (x["lp"], y["d"])]

    def edge_l(x, y):
        return [(x["d"], y["l"]), (x["l"], y["dm"])]

    def edge_u(x, y):
        return [(x["d"], y["u"]), (x["u"], y["dp"])]

    send_f, wait_f, drain_f = sender(0, f["d"], f_dm, f_dp)
    send_b, wait_b, drain_b = sender(1, b["d"], b["dm"], b["dp"])
    send_h, wait_h, drain_h = sender(2, h["d"], h_dm, h_dp)

    product(node(a, a), to_factor(f["d"], k_d, True), send_f)
    product(edge_um(a, a), to_factor(f["um"], keep_um, False))
    product(edge_lp(a, a), to_factor(f["lp"], keep_lp, False))
    product(node(a, f), to_next(b["d"], k_d, BF))
    product(edge_l(a, a), to_factor(f["l"], k_l, False))
    product(edge_u(a, a), to_factor(f["u"], k_u, False))
    product(edge_um(a, f), to_next(b["um"], keep_um, BF))
    product(edge_lp(a, f), to_next(b["lp"], keep_lp, BF))
    drain_f()
    send_b(0)
    send_b(1)

    wait_f(0, 0)
    wait_f(0, 1)
    product(edge_l(a, f), to_next(b["l"], k_l, BF))
    wait_f(1, 0)
    wait_f(1, 1)
    product(edge_u(a, f), to_next(b["u"], k_u, BF))

    product(node(b, b), to_factor(h["d"], k_d, True), send_h)
    wait_b(0, 0)
    wait_b(0, 1)
    product(edge_um(b, b), to_factor(h["um"], keep_um, False))
    product(edge_l(b, b), to_factor(h["l"], k_l, False))
    wait_b(1, 0)
    wait_b(1, 1)
    product(edge_lp(b, b), to_factor(h["lp"], keep_lp, False))
    product(edge_u(b, b), to_factor(h["u"], k_u, False))
    out_l, out_d, out_u = (tile_of(out_ref, k) for k in range(3))
    product(node(b, h), to_next(out_d, k_d, F32))

    def keep_sum(dst):
        def finish(i, j, acc):
            dst[i * H : (i + 1) * H, j * H : (j + 1) * H] = acc

        return finish

    def add_half(dst, x, y, q, mask):
        part = pl.ds(q * H, H)

        def finish(i, j, acc):
            at = (slice(i * H, (i + 1) * H), slice(j * H, (j + 1) * H))
            total = dst[at] + acc
            dst[at] = total if mask is None else 0.5 * total * mask[at].astype(F32)

        product([(x.at[:, part], y.at[part, :])], finish)

    product([(b["d"], h["l"])], keep_sum(out_l))
    product([(b["d"], h["u"])], keep_sum(out_u))
    for q in range(2):
        wait_h(0, q)
        add_half(out_l, b["l"], h_dm, q, k_l if q else None)
        wait_h(1, q)
        add_half(out_u, b["u"], h_dp, q, k_u if q else None)

    drain_b()
    drain_h()
    for cond, make in sends:
        if cond is None:
            make().wait_send()
        else:
            pl.when(cond)(make().wait_send)


def on_device(assembled, dest_group, block_mask):
    tile = pltpu.VMEM((T, T), BF)
    row = pltpu.VMEM((T, 3 * T), BF)
    pair = pltpu.VMEM((T, 2 * T), BF)
    dma = pltpu.SemaphoreType.DMA
    return pl.pallas_call(
        kernel,
        out_shape=jax.ShapeDtypeStruct((T, 3 * T), F32),
        in_specs=[
            pl.BlockSpec(memory_space=pltpu.VMEM),
            pl.BlockSpec(memory_space=pltpu.VMEM),
            pl.BlockSpec(memory_space=pltpu.VMEM),
        ],
        out_specs=pl.BlockSpec(memory_space=pltpu.VMEM),
        scratch_shapes=[
            pltpu.VMEM((2, CHUNK, 3 * T), BF), pltpu.VMEM((CHUNK, 3 * T), BF), pltpu.VMEM((2, CHUNK, 3 * T), BF), row,
            pltpu.VMEM((CB, 128), F32), pltpu.VMEM((CB, 128), F32), pltpu.VMEM((CB, 128), F32),
            row, pair, pair,
            row, pair, pair, row, tile, tile, tile, tile,
            row, pair, pair, row, tile, tile, tile, tile,
            dma, dma, dma((2, PIECES)), dma((2, PIECES)), dma((2, PIECES)), dma((2, PIECES)),
            dma((2, 2 + 2 * PIECES)), dma((2, 2 + 2 * PIECES)), dma((2, 2, PIECES)), dma((3, 2, 2)), dma((3, 2, 2)), dma((2,)), dma((2,)),
        ],
        compiler_params=pltpu.CompilerParams(
            collective_id=0, has_side_effects=True, vmem_limit_bytes=36 * 2**20
        ),
        cost_estimate=pl.CostEstimate(flops=40 * 2 * T**3, bytes_accessed=9 * T * T * 2, transcendentals=0),
        name="sign_steps",
    )(assembled, dest_group, block_mask)


def solution(mesh):
    spec = P(("grp", "pan"), None)
    return jax.shard_map(on_device, mesh=mesh, in_specs=(spec, spec, spec), out_specs=spec, check_vma=False)
```

```python
import functools

import jax
import jax.numpy as jnp
from jax import lax
from jax.experimental import pallas as pl
from jax.experimental.pallas import tpu as pltpu
from jax.sharding import PartitionSpec as P

MESH = pl.DeviceIdType.MESH
ATOM = 64
CB = 8
T = ATOM * CB
CHUNK = 2 * ATOM
H = 256
CUTS = (0, 64, 96, 128)
PIECES = len(CUTS) - 1
BF = jnp.bfloat16
F32 = jnp.float32


def kernel(
    x_ref, dest_ref, mask_ref, out_ref,
    for_far, for_sib, transit, land, mine, mask_l, mask_r, keep, keep_hl, keep_hr,
    a_row, a_hl, a_hr, f_row, f_um, f_lp, f_dm, f_dp,
    b_row, b_hl, b_hr, h_row, h_um, h_lp, h_dm, h_dp,
    sib_s, sib_r, hop_s, hop_r, far_s, far_r, halo_s, halo_r, extra_s, tile_s, tile_r, m_s, m_r,
):
    g = lax.axis_index("grp")
    p = lax.axis_index("pan")
    n = lax.axis_size("pan")
    core = lax.rem(g, 2)
    y_hi = g // 2
    z = lax.rem(p, 4)
    sib = g + 1 - 2 * core
    far = lax.rem(g + 2, 4)
    other_hi = 2 - 2 * y_hi
    wraps = jnp.logical_or(z == 0, z == 3)

    def across(pan):
        return pan + 4 - 8 * lax.rem(pan // 4, 2)

    before, after = lax.rem(p + n - 1, n), lax.rem(p + 1, n)
    inner = across(p)
    left, right = (g, before), (g, after)
    outer_to = (far, inner)
    inner_to = ((g, inner), (sib, inner))

    barrier = pltpu.get_barrier_semaphore()

    def greet(other):
        pl.semaphore_signal(barrier, inc=1, device_id=other, device_id_type=MESH)

    for other in ((sib, p), outer_to, *inner_to, left, right):
        greet(other)

    @pl.when(z == 0)
    def _():
        for who in (g, sib):
            greet((who, across(before)))

    @pl.when(z == 3)
    def _():
        for who in (g, sib):
            greet((who, across(after)))

    def one_hot(rows, cols, of_row, of_col):
        row = of_row(lax.broadcasted_iota(jnp.int32, (rows, cols), 0))
        return (row == of_col(lax.broadcasted_iota(jnp.int32, (rows, cols), 1))).astype(F32)

    eye = one_hot(CB, CB, lambda v: v, lambda v: v)
    lane = lax.broadcasted_iota(jnp.int32, (1, CB), 1)
    key_row = (dest_ref[...] * CB + lane).astype(F32)
    key_col = jnp.sum(eye * key_row, axis=1, keepdims=True)
    rank = jnp.sum((key_col < key_row).astype(F32), axis=0, keepdims=True)
    spread = one_hot(CB, T, lambda v: v, lambda v: v // ATOM)
    goal = jnp.sum(spread * jnp.sum(eye * rank, axis=1, keepdims=True), axis=0, keepdims=True)
    goal = goal * ATOM + (lax.broadcasted_iota(jnp.int32, (1, T), 1) % ATOM).astype(F32)

    def rows_for(group):
        want = (group * CHUNK + lax.broadcasted_iota(jnp.int32, (CHUNK, T), 0)).astype(F32)
        pick = (want == goal).astype(BF)
        return jnp.dot(pick, x_ref[...], preferred_element_type=F32).astype(BF)

    def rows_of(group, t=None):
        if t is None:
            return pl.ds(pl.multiple_of(group * CHUNK, CHUNK), CHUNK)
        return pl.ds(pl.multiple_of(group * CHUNK + CUTS[t], 16), CUTS[t + 1] - CUTS[t])

    sends = []

    def describe(src, dst, ss, rs, to):
        return pltpu.make_async_remote_copy(
            src_ref=src, dst_ref=dst, send_sem=ss, recv_sem=rs, device_id=to, device_id_type=MESH
        )

    def remote(*what):
        copy = describe(*what)
        copy.start()
        sends.append((None, lambda: copy))
        return copy

    def piece(t):
        return pl.ds(CUTS[t], CUTS[t + 1] - CUTS[t])

    def hop(d, t):
        return describe(for_far.at[d, piece(t)], transit.at[d, piece(t)], hop_s.at[d, t], hop_r.at[d, t], outer_to)

    for_far[0] = rows_for(other_hi)
    for_far[1] = rows_for(other_hi + 1)

    @pl.when(wraps)
    def _():
        pl.semaphore_wait(barrier, 8)

    @pl.when(jnp.logical_not(wraps))
    def _():
        pl.semaphore_wait(barrier, 6)

    turns = (core, 1 - core)

    def launch(t):
        for d in turns:
            hop(d, t).start()
            sends.append((None, functools.partial(hop, d, t)))

    for t in range(PIECES):
        launch(t)
    mine[...] = jnp.zeros_like(mine)
    mine[:, : 3 * CB] = mask_ref[...].astype(F32)
    mask_in = (
        remote(mine, mask_l, m_s.at[0], m_r.at[0], right),
        remote(mine, mask_r, m_s.at[1], m_r.at[1], left),
    )
    for_sib[...] = rows_for(sib)
    from_sib = remote(for_sib, land.at[rows_of(g)], sib_s, sib_r, (sib, p))
    land[rows_of(g), :] = rows_for(g)

    right_cols, left_cols = pl.ds(T, 2 * T), pl.ds(0, 2 * T)
    slots = [rows_of(g), rows_of(sib)] + [rows_of(other_hi + c, t) for c in range(2) for t in range(PIECES)]

    def halo(side, slot, rows=None):
        rows = slots[slot] if rows is None else rows
        if side == 0:
            return describe(land.at[rows, right_cols], a_hl.at[rows], halo_s.at[0, slot], halo_r.at[0, slot], right)
        return describe(land.at[rows, left_cols], a_hr.at[rows], halo_s.at[1, slot], halo_r.at[1, slot], left)

    def start_when(cond, copy):
        pl.when(cond)(copy.start)

    def onward(d, t):
        at = rows_of(far, t)
        return describe(transit.at[d, piece(t)], land.at[at], far_s.at[d, t], far_r.at[core, t], (y_hi * 2 + d, inner))

    def extra(side, d, t):
        at = rows_of(far, t)
        to = (y_hi * 2 + d, lax.rem(inner + (1 if side == 0 else n - 1), n))
        cols, dst = ((right_cols, a_hl), (left_cols, a_hr))[side]
        return describe(
            transit.at[d, piece(t), cols], dst.at[at], extra_s.at[side, d, t], halo_r.at[side, 2 + PIECES * core + t], to
        )

    def forward(d, t):
        hop(d, t).wait_recv()
        onward(d, t).start()
        start_when(z == 3, extra(0, d, t))
        start_when(z == 0, extra(1, d, t))

    def settle(c, t):
        slot = 2 + PIECES * c + t
        rows = rows_of(other_hi + c, t)
        describe(transit.at[0, piece(t)], land.at[rows], far_s.at[0, t], far_r.at[c, t], right).wait_recv()
        start_when(z != 3, halo(0, slot, rows))
        start_when(z != 0, halo(1, slot, rows))
        a_row[rows, :] = land[rows, :] * keep[rows, :]

    def expand(block, dst):
        rows = block.shape[0] * ATOM
        cols = block.shape[1] * ATOM
        up = one_hot(rows, CB, lambda v: v // ATOM, lambda v: v).astype(BF)
        over = one_hot(block.shape[1], cols, lambda v: v, lambda v: v // ATOM).astype(BF)
        tall = jnp.dot(up, block.astype(BF), preferred_element_type=F32)
        dst[...] = jnp.dot(tall.astype(BF), over, preferred_element_type=F32).astype(BF)

    def spread_near(slot):
        for side in range(2):
            halo(side, slot).start()

    spread_near(0)
    expand(mine[:, : 3 * CB], keep)
    from_sib.wait_recv()
    spread_near(1)
    mask_in[0].wait_recv()
    mask_in[1].wait_recv()
    expand(mask_l[:, CB : 3 * CB], keep_hl)
    expand(mask_r[:, : 2 * CB], keep_hr)
    for slot in range(2):
        a_row[slots[slot], :] = land[slots[slot], :] * keep[slots[slot], :]

    for t in range(PIECES):
        for k in range(2):
            forward(turns[k], t)
            if t:
                settle(turns[k], t - 1)
    for k in range(2):
        settle(turns[k], PIECES - 1)

    for d in range(2):
        for t in range(PIECES):
            sends.append((None, functools.partial(onward, d, t)))
            sends.append((z == 3, functools.partial(extra, 0, d, t)))
            sends.append((z == 0, functools.partial(extra, 1, d, t)))
    for slot in [0, 1] + [2 + PIECES * c + t for t in range(PIECES) for c in range(2)]:
        for side, (dst, mask) in enumerate(((a_hl, keep_hl), (a_hr, keep_hr))):
            halo(side, slot).wait_recv()
            rows = slots[slot]
            dst[rows, :] = dst[rows, :] * mask[rows, :]
            away = None if slot < 2 else (z != 3, z != 0)[side]
            sends.append((away, functools.partial(halo, side, slot)))
    keep_um = keep_hl.at[:, pl.ds(T, T)]
    keep_lp = keep_hr.at[:, pl.ds(0, T)]

    def tile_of(ref, k):
        return ref.at[:, pl.ds(k * T, T)]

    def product(pairs, finish, after=None):
        for i in range(T // H):
            for j in range(T // H):
                acc = None
                for a, b in pairs:
                    part = jnp.dot(
                        a[i * H : (i + 1) * H, :], b[:, j * H : (j + 1) * H], preferred_element_type=F32
                    )
                    acc = part if acc is None else acc + part
                finish(i, j, acc)
            if after is not None:
                after(i)

    def to_factor(dst, mask, diagonal):
        def finish(i, j, acc):
            at = (slice(i * H, (i + 1) * H), slice(j * H, (j + 1) * H))
            value = acc * mask[at].astype(F32) * (-1.0 / (3.0 * T))
            if diagonal and i == j:
                same = lax.broadcasted_iota(jnp.int32, (H, H), 0) == lax.broadcasted_iota(jnp.int32, (H, H), 1)
                value = jnp.where(same, 3.0 + value, value)
            dst[at] = value.astype(BF)

        return finish

    def to_next(dst, mask, dtype):
        def finish(i, j, acc):
            at = (slice(i * H, (i + 1) * H), slice(j * H, (j + 1) * H))
            dst[at] = (0.5 * acc * mask[at].astype(F32)).astype(dtype)

        return finish

    k_l, k_d, k_u = (tile_of(keep, k) for k in range(3))

    def tiles(row, um_ref, lp_ref, dm_ref, dp_ref):
        return dict(l=tile_of(row, 0), d=tile_of(row, 1), u=tile_of(row, 2), um=um_ref, lp=lp_ref, dm=dm_ref, dp=dp_ref)

    a = tiles(a_row, tile_of(a_hl, 1), tile_of(a_hr, 0), tile_of(a_hl, 0), tile_of(a_hr, 1))
    b = tiles(b_row, tile_of(b_hl, 1), tile_of(b_hr, 0), tile_of(b_hl, 0), tile_of(b_hr, 1))
    f = tiles(f_row, f_um, f_lp, f_dm, f_dp)
    h = tiles(h_row, h_um, h_lp, h_dm, h_dp)

    def sender(k, src, from_left, from_right):
        def swap(side, i):
            half = pl.ds(i * H, H)
            dst, to = ((from_left, right), (from_right, left))[side]
            return describe(src.at[half], dst.at[half], tile_s.at[k, side, i], tile_r.at[k, side, i], to)

        def after(i):
            for side in range(2):
                swap(side, i).start()

        def wait(side, i):
            swap(side, i).wait_recv()

        def drain():
            for i in range(T // H):
                for side in range(2):
                    swap(side, i).wait_send()

        return after, wait, drain

    def node(x, y):
        return [(x["d"], y["d"]), (x["u"], y["lp"]), (x["l"], y["um"])]

    def edge_um(x, y):
        return [(x["dm"], y["um"]), (x["um"], y["d"])]

    def edge_lp(x, y):
        return [(x["dp"], y["lp"]), (x["lp"], y["d"])]

    def edge_l(x, y):
        return [(x["d"], y["l"]), (x["l"], y["dm"])]

    def edge_u(x, y):
        return [(x["d"], y["u"]), (x["u"], y["dp"])]

    send_f, wait_f, drain_f = sender(0, f["d"], f_dm, f_dp)
    send_b, wait_b, drain_b = sender(1, b["d"], b["dm"], b["dp"])
    send_h, wait_h, drain_h = sender(2, h["d"], h_dm, h_dp)

    product(node(a, a), to_factor(f["d"], k_d, True), send_f)
    product(edge_um(a, a), to_factor(f["um"], keep_um, False))
    product(edge_lp(a, a), to_factor(f["lp"], keep_lp, False))
    product(node(a, f), to_next(b["d"], k_d, BF))
    product(edge_l(a, a), to_factor(f["l"], k_l, False))
    product(edge_u(a, a), to_factor(f["u"], k_u, False))
    product(edge_um(a, f), to_next(b["um"], keep_um, BF))
    product(edge_lp(a, f), to_next(b["lp"], keep_lp, BF))
    drain_f()
    send_b(0)
    send_b(1)

    wait_f(0, 0)
    wait_f(0, 1)
    product(edge_l(a, f), to_next(b["l"], k_l, BF))
    wait_f(1, 0)
    wait_f(1, 1)
    product(edge_u(a, f), to_next(b["u"], k_u, BF))

    product(node(b, b), to_factor(h["d"], k_d, True))
    drain_b()
    send_h(0)
    send_h(1)
    wait_b(0, 0)
    wait_b(0, 1)
    product(edge_um(b, b), to_factor(h["um"], keep_um, False))
    product(edge_l(b, b), to_factor(h["l"], k_l, False))
    wait_b(1, 0)
    wait_b(1, 1)
    product(edge_lp(b, b), to_factor(h["lp"], keep_lp, False))
    product(edge_u(b, b), to_factor(h["u"], k_u, False))
    out_l, out_d, out_u = (tile_of(out_ref, k) for k in range(3))
    product(node(b, h), to_next(out_d, k_d, F32))

    def keep_sum(dst):
        def finish(i, j, acc):
            dst[i * H : (i + 1) * H, j * H : (j + 1) * H] = acc

        return finish

    def add_half(dst, x, y, q, mask):
        part = pl.ds(q * H, H)

        def finish(i, j, acc):
            at = (slice(i * H, (i + 1) * H), slice(j * H, (j + 1) * H))
            total = dst[at] + acc
            dst[at] = total if mask is None else 0.5 * total * mask[at].astype(F32)

        product([(x.at[:, part], y.at[part, :])], finish)

    product([(b["d"], h["l"])], keep_sum(out_l))
    product([(b["d"], h["u"])], keep_sum(out_u))
    for q in range(2):
        wait_h(0, q)
        add_half(out_l, b["l"], h_dm, q, k_l if q else None)
        wait_h(1, q)
        add_half(out_u, b["u"], h_dp, q, k_u if q else None)

    drain_h()
    for cond, make in sends:
        if cond is None:
            make().wait_send()
        else:
            pl.when(cond)(make().wait_send)


def on_device(assembled, dest_group, block_mask):
    tile = pltpu.VMEM((T, T), BF)
    row = pltpu.VMEM((T, 3 * T), BF)
    pair = pltpu.VMEM((T, 2 * T), BF)
    dma = pltpu.SemaphoreType.DMA
    return pl.pallas_call(
        kernel,
        out_shape=jax.ShapeDtypeStruct((T, 3 * T), F32),
        in_specs=[
            pl.BlockSpec(memory_space=pltpu.VMEM),
            pl.BlockSpec(memory_space=pltpu.VMEM),
            pl.BlockSpec(memory_space=pltpu.VMEM),
        ],
        out_specs=pl.BlockSpec(memory_space=pltpu.VMEM),
        scratch_shapes=[
            pltpu.VMEM((2, CHUNK, 3 * T), BF), pltpu.VMEM((CHUNK, 3 * T), BF), pltpu.VMEM((2, CHUNK, 3 * T), BF), row,
            pltpu.VMEM((CB, 128), F32), pltpu.VMEM((CB, 128), F32), pltpu.VMEM((CB, 128), F32),
            row, pair, pair,
            row, pair, pair, row, tile, tile, tile, tile,
            row, pair, pair, row, tile, tile, tile, tile,
            dma, dma, dma((2, PIECES)), dma((2, PIECES)), dma((2, PIECES)), dma((2, PIECES)),
            dma((2, 2 + 2 * PIECES)), dma((2, 2 + 2 * PIECES)), dma((2, 2, PIECES)), dma((3, 2, 2)), dma((3, 2, 2)), dma((2,)), dma((2,)),
        ],
        compiler_params=pltpu.CompilerParams(
            collective_id=0, has_side_effects=True, vmem_limit_bytes=36 * 2**20
        ),
        cost_estimate=pl.CostEstimate(flops=40 * 2 * T**3, bytes_accessed=9 * T * T * 2, transcendentals=0),
        name="sign_steps",
    )(assembled, dest_group, block_mask)


def solution(mesh):
    spec = P(("grp", "pan"), None)
    return jax.shard_map(on_device, mesh=mesh, in_specs=(spec, spec, spec), out_specs=spec, check_vma=False)
```
